128 devices in a mesh: prow: 8 (over x, core), pcol: 16 (over y, z).
Axes of the slice: x: 4, y: 4, z: 4, core: 2. Of those that a mesh axis runs over, the one named last changes fastest.
Arguments:
- tile_u: bfloat16 [16, 16, 1024, 512], P('prow', 'pcol'), may hold values from -6 to 6
- tile_v: bfloat16 [16, 16, 1024, 512], P('prow', 'pcol'), may hold values from -6 to 6
- tile_ranks: int32 [16, 16], P('prow', 'pcol'), may hold values from 0 to 3, as said below
- row_u: bfloat16 [16, 1024, 512], P('prow', 'pcol'), may hold values from -6 to 6
- row_v: bfloat16 [16, 1024, 512], P('prow', 'pcol'), may hold values from -6 to 6
- row_ranks: int32 [16], P('prow'), may hold values from 0 to 3, as said below
- col_u: bfloat16 [16, 1024, 512], P('pcol', 'prow'), may hold values from -6 to 6
- col_v: bfloat16 [16, 1024, 512], P('pcol', 'prow'), may hold values from -6 to 6
- col_ranks: int32 [16], P('pcol'), may hold values from 0 to 3, as said below
- diag_tile: float32 [1024, 1024], P('prow', 'pcol'), as said below
- sketch: bfloat16 [1024, 512], replicated, may hold values from -6 to 6
Outputs:
- new_u: bfloat16 [16, 16, 1024, 512], P('prow', 'pcol')
- new_v: bfloat16 [16, 16, 1024, 512], P('prow', 'pcol')
The draws below stay inside these ranges and needn't reach their ends.
Inputs may be any that keep to these rules, and one draw needn't show every extreme that they name: `tile_ranks`: each id names a rank bucket; every draw holds ids 0 and 3. `row_ranks`: each id names a rank bucket; every draw holds ids 0 and 3. `col_ranks`: each id names a rank bucket; every draw holds ids 0 and 3. `diag_tile`: a scaled Matern covariance of 1024 points in the plane plus a nugget on the diagonal; symmetric positive definite with condition number below 25600.
All inputs are finite; a program needn't handle non-finite values.
Results may differ from the reference program's by a relative error of at most 0.014.
Values may be sent and summed in bfloat16 or wider, within the bound.
No kernel may reach another device: no remote copies, remote signals or barrier semaphores. Data moves between devices by JAX's collectives and lax.ppermute only.
A program may use at most 192 MiB of HBM per device.

```python
import math
import jax
import jax.numpy as jnp
from jax import lax

NB = 1024
RMAX = 512
MT = 16
NT = 16


def spread_codes(key, total_codes):
    key_codes, key_top, key_low = jax.random.split(key, 3)
    code_list = jax.random.randint(key_codes, (total_codes,), 0, 4, dtype=jnp.int32)
    top_place = jax.random.randint(key_top, (), 0, total_codes, dtype=jnp.int32)
    low_place = (top_place + 1 + jax.random.randint(key_low, (), 0, total_codes - 1, dtype=jnp.int32)) % total_codes
    position = jnp.arange(total_codes, dtype=jnp.int32)
    code_list = jnp.where(position == top_place, 3, code_list)
    code_list = jnp.where(position == low_place, 0, code_list)
    return code_list


def draw_tile_ranks(key, part):
    return spread_codes(jax.random.fold_in(key, 11), MT * NT).reshape(MT, NT)


def draw_row_ranks(key, part):
    return spread_codes(jax.random.fold_in(key, 12), MT)


def draw_col_ranks(key, part):
    return spread_codes(jax.random.fold_in(key, 13), NT)


def draw_diag_tile(key, part):
    key_first, key_second = jax.random.split(jax.random.fold_in(key, 14))
    coord_first = jax.random.uniform(key_first, (NB,), jnp.float32, 0.0, 1.0)
    coord_second = jax.random.uniform(key_second, (NB,), jnp.float32, 0.0, 1.0)
    length_scale = 0.2
    nugget = 0.1
    spacing = jnp.sqrt(jnp.square(coord_first[:, None] - coord_first[None, :]) + jnp.square(coord_second[:, None] - coord_second[None, :]))
    kernel = jnp.exp(-spacing / length_scale)
    position = jnp.arange(NB, dtype=jnp.int32)
    covariance = kernel + jnp.where(position[:, None] == position[None, :], nugget, 0.0)
    return (8.0 * NB * covariance).astype(jnp.float32)


def block_scale(own_key, dims, cuts, least, largest):
    gain, own = 1.0, jax.random.fold_in(own_key, 6)
    for dim, shards_of in cuts:
        steps = jnp.exp(jax.random.uniform(jax.random.fold_in(own, dim), (shards_of,), jnp.float32, least / len(cuts), largest / len(cuts)))
        gain = gain * jnp.repeat(steps, dims[dim] // shards_of).reshape([-1 if axis == dim else 1 for axis in range(len(dims))])
    return gain


def gaussian(own_key, extent, width, reach, pieces=(), held_as=jnp.bfloat16):
    result = jax.random.normal(own_key, extent, jnp.float32) * width
    if len(pieces) > 0:
        result = block_scale(own_key, extent, pieces, -0.22, 0.18) * result
    return jnp.clip(result, min=-reach, max=reach).astype(held_as)


def setup_inputs(seed: int = 0) -> dict:
    seeds = jax.random.split(jax.random.key(seed), 12)
    return {
        "tile_u": gaussian(seeds[0], (MT, NT, NB, RMAX), 1.0, 6.0, ((0, 8), (1, 16))),
        "tile_v": gaussian(seeds[1], (MT, NT, NB, RMAX), 1.0, 6.0, ((0, 8), (1, 16))),
        "tile_ranks": draw_tile_ranks(jax.random.fold_in(seeds[11], 71), 0),
        "row_u": gaussian(seeds[3], (MT, NB, RMAX), 1.0, 6.0, ((0, 8), (1, 16))),
        "row_v": gaussian(seeds[4], (MT, NB, RMAX), 1.0, 6.0, ((0, 8), (1, 16))),
        "row_ranks": draw_row_ranks(jax.random.fold_in(seeds[11], 71), 0),
        "col_u": gaussian(seeds[6], (NT, NB, RMAX), 1.0, 6.0, ((0, 16), (1, 8))),
        "col_v": gaussian(seeds[7], (NT, NB, RMAX), 1.0, 6.0, ((0, 16), (1, 8))),
        "col_ranks": draw_col_ranks(jax.random.fold_in(seeds[11], 71), 0),
        "diag_tile": draw_diag_tile(jax.random.fold_in(seeds[11], 71), 0),
        "sketch": gaussian(seeds[10], (NB, RMAX), 1.0, 6.0),
    }


def contract_rows(left_side, right_side):
    return lax.dot_general(left_side.astype(jnp.float32), right_side.astype(jnp.float32), (((0,), (0,)), ((), ())), preferred_element_type=jnp.float32)

def rank_mask(bucket_id, rank_width):
    kept_rank = jnp.left_shift(jnp.int32(rank_width // 8), bucket_id.astype(jnp.int32))
    return (jnp.arange(rank_width, dtype=jnp.int32) < kept_rank).astype(jnp.float32)

def panel_solve(diag_factor, factor):
    solved = lax.linalg.triangular_solve(diag_factor, factor.astype(jnp.float32), left_side=True, lower=True)
    return solved.astype(jnp.bfloat16)

def recompress(tile_left, tile_right, mask_tile, row_left, row_right, mask_row, col_left, col_right, mask_col, sketch):
    tile_order = tile_left.shape[0]
    highest = lax.Precision.HIGHEST
    coupling = contract_rows(row_right, col_right) * mask_row[:, None] * mask_col[None, :]
    probe_tile = (contract_rows(tile_right, sketch) * mask_tile[:, None] * mask_tile[None, :]).astype(jnp.bfloat16)
    probe_panel = contract_rows(col_left, sketch)
    probe_update = (jnp.dot(coupling, probe_panel, precision=highest) * mask_tile[None, :]).astype(jnp.bfloat16)
    sampled = jnp.dot(tile_left.astype(jnp.float32), probe_tile.astype(jnp.float32), preferred_element_type=jnp.float32) - jnp.dot(row_left.astype(jnp.float32), probe_update.astype(jnp.float32), preferred_element_type=jnp.float32)
    gram = jnp.dot(sampled.T, sampled, precision=highest) + jnp.diag(1.0 - mask_tile)
    gram_factor = jnp.linalg.cholesky(gram)
    basis = lax.linalg.triangular_solve(gram_factor, sampled, left_side=False, lower=True, transpose_a=True)
    new_left = (basis * math.sqrt(tile_order)).astype(jnp.bfloat16)
    back_tile = (contract_rows(tile_left, new_left) * mask_tile[:, None]).astype(jnp.bfloat16)
    back_row = contract_rows(row_left, new_left)
    back_col = jnp.dot(coupling.T, back_row, precision=highest).astype(jnp.bfloat16)
    summed = jnp.dot(tile_right.astype(jnp.float32), back_tile.astype(jnp.float32), preferred_element_type=jnp.float32) - jnp.dot(col_left.astype(jnp.float32), back_col.astype(jnp.float32), preferred_element_type=jnp.float32)
    new_right = (summed / tile_order).astype(jnp.bfloat16)
    return (new_left, new_right)

def reference(tile_u, tile_v, tile_ranks, row_u, row_v, row_ranks, col_u, col_v, col_ranks, diag_tile, sketch):
    rank_width = tile_u.shape[3]
    diag_factor = jnp.linalg.cholesky(diag_tile)
    row_solved = lax.map(lambda factor: panel_solve(diag_factor, factor), row_v)
    col_solved = lax.map(lambda factor: panel_solve(diag_factor, factor), col_v)

    def one_row(row_index):

        def one_col(col_index):
            return recompress(tile_u[row_index, col_index], tile_v[row_index, col_index], rank_mask(tile_ranks[row_index, col_index], rank_width), row_u[row_index], row_solved[row_index], rank_mask(row_ranks[row_index], rank_width), col_u[col_index], col_solved[col_index], rank_mask(col_ranks[col_index], rank_width), sketch)
        return lax.map(one_col, jnp.arange(NT, dtype=jnp.int32))
    new_u, new_v = lax.map(one_row, jnp.arange(MT, dtype=jnp.int32))
    return (new_u, new_v)
```

```python
import math

import jax
import jax.numpy as jnp
from jax import lax
from jax.experimental import pallas as pl
from jax.experimental.pallas import tpu as pltpu
from jax.sharding import PartitionSpec as P

B = 128
S = 8
f32 = jnp.float32
bf16 = jnp.bfloat16

def split(x, pieces):
    out = []
    for t in range(pieces):
        part = x.astype(bf16)
        out.append(part)
        if t + 1 < pieces:
            x = x - part.astype(f32)
    return out

def dot(a, b, ca=1, cb=0):
    return lax.dot_general(a, b, (((ca,), (cb,)), ((), ())), preferred_element_type=f32)

def rowb(x, k):
    return jnp.broadcast_to(x[k:k + 1, :], (S, B))

def laneb(x, j):
    return jnp.broadcast_to(x[:, j:j + 1], (S, B))

def eliminate_panel(rows, j, lane, sub):
    inside = (lane >= j) & (lane < j + S)
    cols = [laneb(rows, j + k) for k in range(S)]
    kept = jnp.where(inside, (lane - j == sub).astype(f32), rows)
    pivots = None
    upper, lines, inverses = [], [], []
    for k in range(S):
        pivot = rowb(cols[k], k)
        inverse = 1.0 / pivot
        pivots = pivot if pivots is None else jnp.where(sub == k, pivot, pivots)
        line = rowb(kept, k)
        across = [rowb(cols[m], k) for m in range(k + 1, S)]
        for m in range(k + 1, S):
            cols[m] = cols[m] - (cols[k] * across[m - k - 1]) * inverse
        kept = kept - jnp.where(sub > k, cols[k], 0.0) * (line * inverse)
        upper.append(across)
        lines.append(line)
        inverses.append(inverse)
    return kept * lax.rsqrt(pivots), upper, lines, inverses, inside

def eliminate_below(rows, j, upper, lines, inverses, inside):
    cols = [laneb(rows, j + k) for k in range(S)]
    rest = jnp.where(inside, 0.0, rows)
    for k in range(S):
        weight = cols[k] * inverses[k]
        for m in range(k + 1, S):
            cols[m] = cols[m] - weight * upper[k][m - k - 1]
        rest = rest - weight * lines[k]
    return rest

def block_inverse(ref):
    lane = lax.broadcasted_iota(jnp.int32, (S, B), 1)
    sub = lax.broadcasted_iota(jnp.int32, (S, B), 0)
    current = ref[0:S, :]
    for j in range(0, B, S):
        done, *rule = eliminate_panel(current, j, lane, sub)
        ref[j:j + S, :] = jnp.where(lane <= j + sub, done, 0.0)
        for i in range(j + S, B, S):
            new = eliminate_below(ref[i:i + S, :], j, *rule)
            if i == j + S:
                current = new
            else:
                ref[i:i + S, :] = new
        yield

def pairs_left(p, axis):
    return jnp.concatenate([p[0], p[0], p[1], p[1], p[0], p[2]], axis=axis)

def pairs_right(p, axis):
    return jnp.concatenate([p[0], p[1], p[0], p[1], p[2], p[0]], axis=axis)

def block_step(k, read, work, diag, pieces, out_rows, n):
    nb = n // B
    r0 = k * B
    own = diag[...]
    own_parts = split(own, 3)
    left = pairs_left(own_parts, 1)

    def line(lo, hi):
        g = dot(left, pairs_right(split(read(r0, lo, hi), 3), 0))
        for t, part in enumerate(split(g, 3)):
            pieces[t, :, lo:hi] = part
        return g

    def shrink(i, lo, hi, zero=False, dest=None):
        a = pairs_left([pieces[t, :, i * B:(i + 1) * B] for t in range(3)], 0)
        b = pairs_right([pieces[t, :, lo:hi] for t in range(3)], 0)
        d = dot(a, b, 0, 0)
        new = -d if zero else read(i * B, lo, hi) - d
        if dest is None:
            work[i * B:(i + 1) * B, lo:hi] = new
        else:
            dest[...] = new

    pending = []
    if k + 1 < nb:
        line(r0 + B, r0 + 2 * B)
        shrink(k + 1, r0 + B, r0 + 2 * B, dest=diag)
        for t, part in enumerate(own_parts):
            pieces[t, :, r0:r0 + B] = part
    out_rows(k, r0, own)
    if k > 0:
        pending.append(lambda: out_rows(k, 0, line(0, r0)))
    if k + 2 < nb:
        pending.append(lambda: line(r0 + 2 * B, n))
    for i in range(k + 1, nb):
        if i > k + 1:
            pending.append(lambda i=i: shrink(i, i * B, n))
        elif i + 1 < nb:
            pending.append(lambda i=i: shrink(i, i * B + B, n))
        pending.append(lambda i=i: shrink(i, r0, r0 + B, zero=True))
        if k > 0:
            pending.append(lambda i=i: shrink(i, 0, r0))
    return pending

def factor_inverse(src, work, diag, pieces, out_rows, n):
    nb = n // B
    diag[...] = src(0, 0, B)

    def again(row, lo, hi):
        return work[row:row + B, lo:hi]

    pending = []
    for k in range(nb):
        step = block_inverse(diag)
        panels = B // S
        done = 0
        for p in range(panels):
            next(step)
            upto = (p + 1) * len(pending) // (panels - 1) if p < panels - 1 else len(pending)
            for t in range(done, min(upto, len(pending))):
                pending[t]()
            done = max(done, min(upto, len(pending)))
            yield
        pending = block_step(k, src if k == 0 else again, work, diag, pieces, out_rows, n)
    for t in pending:
        t()
    yield

def drive(gens):
    gens = list(gens)
    while gens:
        alive = []
        for g in gens:
            try:
                next(g)
                alive.append(g)
            except StopIteration:
                pass
        gens = alive


def diag_kernel(strips, high, low, work, diag, pieces):
    n = high.shape[0]
    high[...] = jnp.zeros(high.shape, bf16)
    low[...] = jnp.zeros(low.shape, bf16)

    def source(row, lo, hi):
        return jnp.concatenate([strips[q, row:row + B, :] for q in range(lo // B, hi // B)], axis=1)

    def out_rows(k, lo, value):
        parts = split(value, 2)
        for ref, part in zip((high, low), parts):
            ref[k * B:(k + 1) * B, lo:lo + value.shape[1]] = part

    drive([factor_inverse(source, work, diag, pieces, out_rows, n)])


def diag_inverse(strips):
    n = strips.shape[1]
    return pl.pallas_call(
        diag_kernel,
        out_shape=[jax.ShapeDtypeStruct((n, n), bf16)] * 2,
        scratch_shapes=[pltpu.VMEM((n, n), f32), pltpu.VMEM((B, B), f32), pltpu.VMEM((3, B, n), bf16)],
        compiler_params=pltpu.CompilerParams(vmem_limit_bytes=28 << 20),
        cost_estimate=pl.CostEstimate(flops=40 * 10**9, bytes_accessed=64 << 20, transcendentals=0),
        name="diag_inverse",
    )(strips)


C = 256


def update_kernel(
    tile_ranks, row_ranks, col_ranks,
    tile_u, tile_v, row_u, row_v, col_u, col_v, sketch, high, low,
    new_u, new_v,
    row_s, col_s, coup, panel, mids, samp, grams, work, diag, pieces, fac, backs,
):
    n, r = tile_u.shape[1:]
    tiles = tile_u.shape[0]
    chunks = n // C
    strip = row_u.shape[2]
    per = C // strip

    def live(bucket):
        return jnp.left_shift(jnp.int32(r // 8), bucket)

    def lanes(count, rows):
        return lax.broadcasted_iota(jnp.int32, (rows, r), 1) < count

    def subs(count, start, rows, width):
        return lax.broadcasted_iota(jnp.int32, (rows, width), 0) + start < count

    def row_chunk(ref, t, c):
        return ref[pl.ds(c * per, per), t].reshape(C, r)

    def rows_all(ref, t):
        return ref[:, t].reshape(n, r)

    for b in range(chunks):
        k = (b + 1) * C
        left = jnp.concatenate([high[b * C:k, :k], low[b * C:k, :k]], axis=1)

        def solve(t, carry):
            v = row_v[0:k // strip, t].reshape(k, r)
            row_s[t, b * C:k, :] = dot(left, jnp.concatenate([v, v], axis=0)).astype(bf16)
            return carry

        lax.fori_loop(0, tiles, solve, 0)
        v = col_v[0:k, :]
        col_s[b * C:k, :] = dot(left, jnp.concatenate([v, v], axis=0)).astype(bf16)

    for b in range(r // C):
        part = dot(col_u[:, b * C:(b + 1) * C], sketch[...], 0, 0)
        for q, piece in enumerate(split(part, 2)):
            panel[q, b * C:(b + 1) * C, :] = piece

    col_live = live(col_ranks[0])

    def first(t, carry):
        row_live = live(row_ranks[t])
        tile_live = live(tile_ranks[t])
        for b in range(r // C):
            sl = slice(b * C, (b + 1) * C)
            c = dot(row_s[t, :, sl], col_s[...], 0, 0)
            keep = subs(row_live, b * C, C, r) & lanes(col_live, C)
            c = split(jnp.where(keep, c, 0.0), 2)
            for q in range(2):
                coup[t, q, sl, :] = c[q]
            left = jnp.concatenate([c[0], c[0], c[1]], axis=1)
            right = jnp.concatenate([panel[0], panel[1], panel[0]], axis=0)
            u = jnp.where(lanes(tile_live, C), dot(left, right), 0.0)
            mids[r + b * C:r + (b + 1) * C, :] = (-u).astype(bf16)
            v = dot(tile_v[t, :, sl], sketch[...], 0, 0)
            keep = subs(tile_live, b * C, C, r) & lanes(tile_live, C)
            mids[sl, :] = jnp.where(keep, v, 0.0).astype(bf16)
        for b in range(chunks):
            sl = slice(b * C, (b + 1) * C)
            left = jnp.concatenate([tile_u[t, sl, :], row_u[b * per:(b + 1) * per, t].reshape(C, r)], axis=1)
            for q, piece in enumerate(split(dot(left, mids[...]), 2)):
                samp[t, q, sl, :] = piece
        for b in range(r // C):
            sl = slice(b * C, (b + 1) * C)
            lo = b * C
            left = jnp.concatenate([samp[t, 0, :, sl], samp[t, 0, :, sl], samp[t, 1, :, sl], samp[t, 1, :, sl]], axis=0)
            right = jnp.concatenate([samp[t, 0, :, lo:], samp[t, 1, :, lo:], samp[t, 0, :, lo:], samp[t, 1, :, lo:]], axis=0)
            g = dot(left, right, 0, 0)
            row = lax.broadcasted_iota(jnp.int32, g.shape, 0)
            one = (row == lax.broadcasted_iota(jnp.int32, g.shape, 1)) & (row + lo >= tile_live)
            grams[t, sl, lo:] = g + one.astype(f32)
        return carry

    lax.fori_loop(0, tiles, first, 0)

    fac[...] = jnp.zeros(fac.shape, bf16)

    def factor(t):
        def source(row, lo, hi):
            return grams[t, row:row + B, lo:hi]

        def out_rows(k, lo, value):
            for q, part in enumerate(split(value, 2)):
                fac[t, q, k * B:(k + 1) * B, lo:lo + value.shape[1]] = part

        return factor_inverse(source, work.at[t], diag.at[t], pieces.at[t], out_rows, r)

    drive([factor(t) for t in range(tiles)])

    scale = math.sqrt(n)

    def last(t, carry):
        tile_live = live(tile_ranks[t])
        for h in range(r // C):
            hs = slice(h * C, (h + 1) * C)
            k = (h + 1) * C
            right = jnp.concatenate([fac[t, 0, hs, :k], fac[t, 0, hs, :k], fac[t, 1, hs, :k]], axis=1)
            for b in range(chunks):
                sl = slice(b * C, (b + 1) * C)
                left = jnp.concatenate([samp[t, 0, sl, :k], samp[t, 1, sl, :k], samp[t, 0, sl, :k]], axis=1)
                new_u[t, sl, hs] = (dot(left, right, 1, 1) * scale).astype(bf16)
        for b in range(r // C):
            sl = slice(b * C, (b + 1) * C)
            v = dot(tile_u[t, :, sl], new_u[t], 0, 0)
            mids[sl, :] = jnp.where(subs(tile_live, b * C, C, r), v, 0.0).astype(bf16)
            v = dot(row_u[:, t, :, sl].reshape(n, C), new_u[t], 0, 0)
            for q, piece in enumerate(split(v, 2)):
                backs[q, sl, :] = piece
        for b in range(r // C):
            sl = slice(b * C, (b + 1) * C)
            left = jnp.concatenate([coup[t, 0, :, sl], coup[t, 0, :, sl], coup[t, 1, :, sl]], axis=0)
            right = jnp.concatenate([backs[0], backs[1], backs[0]], axis=0)
            mids[r + b * C:r + (b + 1) * C, :] = (-dot(left, right, 0, 0)).astype(bf16)
        for b in range(chunks):
            sl = slice(b * C, (b + 1) * C)
            left = jnp.concatenate([tile_v[t, sl, :], col_u[sl, :]], axis=1)
            new_v[t, sl, :] = (dot(left, mids[...]) * (1.0 / n)).astype(bf16)
        return carry

    lax.fori_loop(0, tiles, last, 0)


def update_tiles(tile_ranks, row_ranks, col_ranks, tile_u, tile_v, row_u, row_v, col_u, col_v, sketch, high, low):
    tiles, n, r = tile_u.shape
    smem = pl.BlockSpec(memory_space=pltpu.SMEM)
    vmem = pl.BlockSpec(memory_space=pltpu.VMEM)
    return pl.pallas_call(
        update_kernel,
        out_shape=[jax.ShapeDtypeStruct((tiles, n, r), bf16)] * 2,
        in_specs=[smem] * 3 + [vmem] * 9,
        out_specs=[vmem] * 2,
        scratch_shapes=[
            pltpu.VMEM((tiles, n, r), bf16),
            pltpu.VMEM((n, r), bf16),
            pltpu.VMEM((tiles, 2, r, r), bf16),
            pltpu.VMEM((2, r, r), bf16),
            pltpu.VMEM((2 * r, r), bf16),
            pltpu.VMEM((tiles, 2, n, r), bf16),
            pltpu.VMEM((tiles, r, r), f32),
            pltpu.VMEM((tiles, r, r), f32),
            pltpu.VMEM((tiles, B, B), f32),
            pltpu.VMEM((tiles, 3, B, r), bf16),
            pltpu.VMEM((tiles, 2, r, r), bf16),
            pltpu.VMEM((2, r, r), bf16),
        ],
        compiler_params=pltpu.CompilerParams(vmem_limit_bytes=56 << 20),
        cost_estimate=pl.CostEstimate(flops=60 * 10**9, bytes_accessed=64 << 20, transcendentals=0),
        name="update_tiles",
    )(tile_ranks, row_ranks, col_ranks, tile_u, tile_v, row_u, row_v, col_u, col_v, sketch, high, low)


def on_device(
    tile_u, tile_v, tile_ranks, row_u, row_v, row_ranks, col_u, col_v, col_ranks, diag_tile, sketch
):
    n, r = tile_u.shape[2:]
    strips = lax.all_gather(diag_tile.T, ("prow", "pcol"), axis=0, tiled=False)
    strips = strips.reshape(n // B, n, B)
    high, low = diag_inverse(strips)
    row_left = lax.all_gather(row_u, "pcol", axis=0, tiled=False)
    row_raw = lax.all_gather(row_v, "pcol", axis=0, tiled=False)
    col_left = lax.all_gather(col_u[0], "prow", axis=0, tiled=True)
    col_raw = lax.all_gather(col_v[0], "prow", axis=0, tiled=True)
    new_u, new_v = update_tiles(
        tile_ranks[:, 0], row_ranks, col_ranks, tile_u[:, 0], tile_v[:, 0],
        row_left, row_raw, col_left, col_raw, sketch, high, low,
    )
    return new_u[:, None], new_v[:, None]


def solution(mesh):
    in_specs = (
        P("prow", "pcol", None, None),
        P("prow", "pcol", None, None),
        P("prow", "pcol"),
        P("prow", "pcol", None),
        P("prow", "pcol", None),
        P("prow"),
        P("pcol", "prow", None),
        P("pcol", "prow", None),
        P("pcol"),
        P("prow", "pcol"),
        P(),
    )
    out_specs = (P("prow", "pcol", None, None), P("prow", "pcol", None, None))
    return jax.shard_map(
        on_device, mesh=mesh, in_specs=in_specs, out_specs=out_specs, check_vma=False
    )
```

```python
import math

import jax
import jax.numpy as jnp
from jax import lax
from jax.experimental import pallas as pl
from jax.experimental.pallas import tpu as pltpu
from jax.sharding import PartitionSpec as P

B = 128
S = 8
f32 = jnp.float32
bf16 = jnp.bfloat16

def split(x, pieces):
    out = []
    for t in range(pieces):
        part = x.astype(bf16)
        out.append(part)
        if t + 1 < pieces:
            x = x - part.astype(f32)
    return out

def dot(a, b, ca=1, cb=0):
    return lax.dot_general(a, b, (((ca,), (cb,)), ((), ())), preferred_element_type=f32)

def rowb(x, k):
    return jnp.broadcast_to(x[k:k + 1, :], (S, B))

def laneb(x, j):
    return jnp.broadcast_to(x[:, j:j + 1], (S, B))

def eliminate_panel(rows, j, lane, sub):
    inside = (lane >= j) & (lane < j + S)
    cols = [laneb(rows, j + k) for k in range(S)]
    kept = jnp.where(inside, (lane - j == sub).astype(f32), rows)
    pivots = None
    upper, lines, inverses = [], [], []
    for k in range(S):
        pivot = rowb(cols[k], k)
        inverse = 1.0 / pivot
        pivots = pivot if pivots is None else jnp.where(sub == k, pivot, pivots)
        line = rowb(kept, k)
        across = [rowb(cols[m], k) for m in range(k + 1, S)]
        for m in range(k + 1, S):
            cols[m] = cols[m] - (cols[k] * across[m - k - 1]) * inverse
        kept = kept - jnp.where(sub > k, cols[k], 0.0) * (line * inverse)
        upper.append(across)
        lines.append(line)
        inverses.append(inverse)
    return kept * lax.rsqrt(pivots), upper, lines, inverses, inside

def eliminate_below(rows, j, upper, lines, inverses, inside):
    cols = [laneb(rows, j + k) for k in range(S)]
    rest = jnp.where(inside, 0.0, rows)
    for k in range(S):
        weight = cols[k] * inverses[k]
        for m in range(k + 1, S):
            cols[m] = cols[m] - weight * upper[k][m - k - 1]
        rest = rest - weight * lines[k]
    return rest

def block_inverse(ref):
    lane = lax.broadcasted_iota(jnp.int32, (S, B), 1)
    sub = lax.broadcasted_iota(jnp.int32, (S, B), 0)
    current = ref[0:S, :]
    for j in range(0, B, S):
        done, *rule = eliminate_panel(current, j, lane, sub)
        ref[j:j + S, :] = jnp.where(lane <= j + sub, done, 0.0)
        for i in range(j + S, B, S):
            new = eliminate_below(ref[i:i + S, :], j, *rule)
            if i == j + S:
                current = new
            else:
                ref[i:i + S, :] = new
        yield

def look_inverse(ref):
    lane = lax.broadcasted_iota(jnp.int32, (S, B), 1)
    sub = lax.broadcasted_iota(jnp.int32, (S, B), 0)
    rows = ref[0:S, :]
    cols = [laneb(rows, k) for k in range(S)]
    for j in range(0, B, S):
        more = j + S < B
        inside = (lane >= j) & (lane < j + S)
        kept = jnp.where(inside, (lane - j == sub).astype(f32), rows)
        if more:
            below = ref[j + S:j + 2 * S, :]
            cross = [laneb(below, j + k) for k in range(S)]
            ahead = [laneb(below, j + S + k) for k in range(S)]
            rest = jnp.where(inside, 0.0, below)
        pivots = None
        upper, lines, inverses = [], [], []
        for k in range(S):
            pivot = rowb(cols[k], k)
            inverse = 1.0 / pivot
            pivots = pivot if pivots is None else jnp.where(sub == k, pivot, pivots)
            across = [rowb(cols[m], k) for m in range(k + 1, S)]
            for m in range(k + 1, S):
                cols[m] = cols[m] - (cols[k] * across[m - k - 1]) * inverse
            line = rowb(kept, k)
            if more:
                weight = cross[k] * inverse
                own = cross[k]
                for m in range(k + 1, S):
                    cross[m] = cross[m] - (own * across[m - k - 1]) * inverse
                for m in range(S):
                    ahead[m] = ahead[m] - (own * rowb(own, m)) * inverse
                rest = rest - weight * line
            kept = kept - jnp.where(sub > k, cols[k], 0.0) * (line * inverse)
            upper.append(across)
            lines.append(line)
            inverses.append(inverse)
        ref[j:j + S, :] = jnp.where(lane <= j + sub, kept * lax.rsqrt(pivots), 0.0)
        for i in range(j + 2 * S, B, S):
            ref[i:i + S, :] = eliminate_below(ref[i:i + S, :], j, upper, lines, inverses, inside)
        if more:
            cols, rows = ahead, rest
        yield

def pairs_left(p, axis):
    return jnp.concatenate([p[0], p[0], p[1], p[1], p[0], p[2]], axis=axis)

def pairs_right(p, axis):
    return jnp.concatenate([p[0], p[1], p[0], p[1], p[2], p[0]], axis=axis)

def block_step(k, read, work, diag, pieces, out_rows, n):
    nb = n // B
    r0 = k * B
    own = diag[...]
    own_parts = split(own, 3)
    left = pairs_left(own_parts, 1)

    def line(lo, hi):
        g = dot(left, pairs_right(split(read(r0, lo, hi), 3), 0))
        for t, part in enumerate(split(g, 3)):
            pieces[t, :, lo:hi] = part
        return g

    def shrink(i, lo, hi, zero=False, dest=None):
        a = pairs_left([pieces[t, :, i * B:(i + 1) * B] for t in range(3)], 0)
        b = pairs_right([pieces[t, :, lo:hi] for t in range(3)], 0)
        d = dot(a, b, 0, 0)
        new = -d if zero else read(i * B, lo, hi) - d
        if dest is None:
            work[i * B:(i + 1) * B, lo:hi] = new
        else:
            dest[...] = new

    pending = []
    if k + 1 < nb:
        line(r0 + B, r0 + 2 * B)
        shrink(k + 1, r0 + B, r0 + 2 * B, dest=diag)
        for t, part in enumerate(own_parts):
            pieces[t, :, r0:r0 + B] = part
    out_rows(k, r0, own)
    if k > 0:
        pending.append(lambda: out_rows(k, 0, line(0, r0)))
    if k + 2 < nb:
        pending.append(lambda: line(r0 + 2 * B, n))
    for i in range(k + 1, nb):
        if i > k + 1:
            pending.append(lambda i=i: shrink(i, i * B, n))
        elif i + 1 < nb:
            pending.append(lambda i=i: shrink(i, i * B + B, n))
        pending.append(lambda i=i: shrink(i, r0, r0 + B, zero=True))
        if k > 0:
            pending.append(lambda i=i: shrink(i, 0, r0))
    return pending

def factor_inverse(src, work, diag, pieces, out_rows, n, leaf):
    nb = n // B
    diag[...] = src(0, 0, B)

    def again(row, lo, hi):
        return work[row:row + B, lo:hi]

    pending = []
    for k in range(nb):
        step = leaf(diag)
        panels = B // S
        done = 0
        for p in range(panels):
            next(step)
            upto = (p + 1) * len(pending) // (panels - 1) if p < panels - 1 else len(pending)
            for t in range(done, min(upto, len(pending))):
                pending[t]()
            done = max(done, min(upto, len(pending)))
            yield
        pending = block_step(k, src if k == 0 else again, work, diag, pieces, out_rows, n)
    for t in pending:
        t()
    yield

def drive(gens):
    gens = list(gens)
    while gens:
        alive = []
        for g in gens:
            try:
                next(g)
                alive.append(g)
            except StopIteration:
                pass
        gens = alive


def piece_slot(pos, index):
    return ((pos[2] - index // 4) & 3) * 4 + ((pos[3] - index % 4) & 3)


def diag_kernel(pos_ref, *refs):
    arrays, (high_out, low_out, high, low, strips, work, diag, pieces, sems) = refs[:8], refs[8:]
    n = high.shape[0]
    copies = [pltpu.make_async_copy(a, strips.at[i], sems.at[i]) for i, a in enumerate(arrays)]
    for copy in copies:
        copy.start()
    high[...] = jnp.zeros(high.shape, bf16)
    low[...] = jnp.zeros(low.shape, bf16)
    pos = [pos_ref[i] for i in range(4)]
    for copy in copies:
        copy.wait()

    def source(row, lo, hi):
        across = []
        for q in range(lo // B, hi // B):
            slot = ((pos[1] + q) & 1) * 4 + ((pos[0] - q // 2) & 3)
            down = [strips[slot, piece_slot(pos, row // 64 + h)] for h in range(2)]
            across.append(jnp.concatenate(down, axis=0))
        return jnp.concatenate(across, axis=1) if len(across) > 1 else across[0]

    def out_rows(k, lo, value):
        parts = split(value, 2)
        for ref, part in zip((high, low), parts):
            ref[k * B:(k + 1) * B, lo:lo + value.shape[1]] = part
        if lo == 0:
            own = pl.ds(k * B, B)
            for h, (ref, out) in enumerate(((high, high_out), (low, low_out))):
                stores.append(pltpu.make_async_copy(ref.at[own], out.at[own], sems.at[8 + 2 * k + h]))
                stores[-1].start()

    stores = []
    drive([factor_inverse(source, work, diag, pieces, out_rows, n, look_inverse)])
    for copy in stores:
        copy.wait()


def diag_inverse(pos, arrays):
    n = 1024
    return pl.pallas_call(
        diag_kernel,
        out_shape=[jax.ShapeDtypeStruct((n, n), bf16)] * 2,
        in_specs=[pl.BlockSpec(memory_space=pltpu.SMEM)] + [pl.BlockSpec(memory_space=pltpu.HBM)] * 8,
        out_specs=[pl.BlockSpec(memory_space=pltpu.HBM)] * 2,
        scratch_shapes=[
            pltpu.VMEM((n, n), bf16),
            pltpu.VMEM((n, n), bf16),
            pltpu.VMEM((8, 16, n // 16, B), f32),
            pltpu.VMEM((n, n), f32),
            pltpu.VMEM((B, B), f32),
            pltpu.VMEM((3, B, n), bf16),
            pltpu.SemaphoreType.DMA((8 + 2 * (n // B),)),
        ],
        compiler_params=pltpu.CompilerParams(vmem_limit_bytes=58 << 20),
        cost_estimate=pl.CostEstimate(flops=40 * 10**9, bytes_accessed=64 << 20, transcendentals=0),
        name="diag_inverse",
    )(pos, *arrays)


C = 256


def live(bucket, r):
    return jnp.left_shift(jnp.int32(r // 8), bucket)


def lanes(count, rows, r):
    return lax.broadcasted_iota(jnp.int32, (rows, r), 1) < count


def subs(count, start, rows, width):
    return lax.broadcasted_iota(jnp.int32, (rows, width), 0) + start < count


def couple_kernel(
    pos_ref, tile_ranks, row_ranks, col_ranks,
    tile_v_in, row_own, row_1, row_2, row_3, col_v_in, sketch_in, high_in, low_in,
    coup, probe,
    tile_v, row_v, col_v, sketch, high, low, row_s, col_s, sems,
):
    n, r = tile_v.shape[1:]
    tiles = tile_v.shape[0]
    chunks = n // C
    strip = row_v.shape[2]
    halves = r // C
    pos = [pos_ref[i] for i in range(4)]
    early = [
        pltpu.make_async_copy(sketch_in, sketch, sems.at[0]),
        pltpu.make_async_copy(tile_v_in, tile_v, sems.at[1]),
    ]
    middle = [
        pltpu.make_async_copy(high_in, high, sems.at[2]),
        pltpu.make_async_copy(low_in, low, sems.at[3]),
        pltpu.make_async_copy(col_v_in, col_v, sems.at[4]),
    ]
    for sz, ref in enumerate((row_own, row_1, row_2, row_3)):
        for sy in range(4):
            place = ((pos[2] - sy) & 3) * 4 + ((pos[3] - sz) & 3)
            middle.append(pltpu.make_async_copy(ref.at[sy], row_v.at[place], sems.at[5 + sz * 4 + sy]))
    for copy in early + middle:
        copy.start()
    for copy in early:
        copy.wait()

    def project(t, carry):
        tile_live = live(tile_ranks[t], r)
        for b in range(halves):
            sl = slice(b * C, (b + 1) * C)
            v = dot(tile_v[t, :, sl], sketch[...], 0, 0)
            keep = subs(tile_live, b * C, C, r) & lanes(tile_live, C, r)
            probe[t, sl, :] = jnp.where(keep, v, 0.0).astype(bf16)
        return carry

    lax.fori_loop(0, tiles, project, 0)
    for copy in middle:
        copy.wait()

    for b in range(chunks):
        k = (b + 1) * C
        left = jnp.concatenate([high[b * C:k, :k], low[b * C:k, :k]], axis=1)

        def solve(t, carry):
            v = row_v[0:k // strip, t].reshape(k, r)
            row_s[t, b * C:k, :] = dot(left, jnp.concatenate([v, v], axis=0)).astype(bf16)
            return carry

        lax.fori_loop(0, tiles, solve, 0)
        v = col_v[0:k, :]
        col_s[b * C:k, :] = dot(left, jnp.concatenate([v, v], axis=0)).astype(bf16)

    col_live = live(col_ranks[0], r)

    def couple(t, carry):
        row_live = live(row_ranks[t], r)
        for b in range(halves):
            sl = slice(b * C, (b + 1) * C)
            c = dot(row_s[t, :, sl], col_s[...], 0, 0)
            keep = subs(row_live, b * C, C, r) & lanes(col_live, C, r)
            coup[t, sl, :] = jnp.where(keep, c, 0.0).astype(bf16)
        return carry

    lax.fori_loop(0, tiles, couple, 0)


def couple_tiles(pos, tile_ranks, row_ranks, col_ranks, tile_v, rows, col_v, sketch, high, low):
    tiles, n, r = tile_v.shape
    smem = pl.BlockSpec(memory_space=pltpu.SMEM)
    vmem = pl.BlockSpec(memory_space=pltpu.VMEM)
    kept = pl.BlockSpec(memory_space=pltpu.HBM)
    return pl.pallas_call(
        couple_kernel,
        out_shape=[jax.ShapeDtypeStruct((tiles, r, r), bf16)] * 2,
        in_specs=[smem] * 4 + [kept] * 9,
        out_specs=[vmem] * 2,
        scratch_shapes=[
            pltpu.VMEM((tiles, n, r), bf16),
            pltpu.VMEM((16, tiles, n // 16, r), bf16),
            pltpu.VMEM((n, r), bf16),
            pltpu.VMEM((n, r), bf16),
            pltpu.VMEM((n, n), bf16),
            pltpu.VMEM((n, n), bf16),
            pltpu.VMEM((tiles, n, r), bf16),
            pltpu.VMEM((n, r), bf16),
            pltpu.SemaphoreType.DMA((21,)),
        ],
        compiler_params=pltpu.CompilerParams(vmem_limit_bytes=58 << 20),
        cost_estimate=pl.CostEstimate(flops=12 * 10**9, bytes_accessed=20 << 20, transcendentals=0),
        name="couple_tiles",
    )(pos, tile_ranks, row_ranks, col_ranks, tile_v, *rows, col_v, sketch, high, low)


def update_kernel(
    tile_ranks,
    tile_u_in, tile_v_in, row_u_in, col_u_in, sketch_in, coup_in, probe_in,
    new_u, new_v,
    tile_u, tile_v, row_u, col_u, sketch, coup,
    panel, mids, samp, grams, work, diag, pieces, fac, backs, sems,
):
    n, r = tile_u.shape[1:]
    tiles = tile_u.shape[0]
    chunks = n // C
    strip = row_u.shape[2]
    per = C // strip
    halves = r // C
    copies = [
        pltpu.make_async_copy(sketch_in, sketch, sems.at[0]),
        pltpu.make_async_copy(col_u_in, col_u, sems.at[1]),
        pltpu.make_async_copy(coup_in, coup, sems.at[2]),
        pltpu.make_async_copy(probe_in.at[0], mids.at[0, 0:r], sems.at[3]),
        pltpu.make_async_copy(probe_in.at[1], mids.at[1, 0:r], sems.at[4]),
        pltpu.make_async_copy(tile_u_in, tile_u, sems.at[5]),
        pltpu.make_async_copy(row_u_in, row_u, sems.at[6]),
        pltpu.make_async_copy(tile_v_in, tile_v, sems.at[7]),
    ]
    for copy in copies:
        copy.start()
    fac[...] = jnp.zeros(fac.shape, bf16)
    copies[0].wait()
    copies[1].wait()
    for b in range(halves):
        sl = slice(b * C, (b + 1) * C)
        panel[sl, :] = dot(col_u[:, sl], sketch[...], 0, 0).astype(bf16)
    copies[2].wait()
    copies[3].wait()
    copies[4].wait()

    def refine(t, carry):
        tile_live = live(tile_ranks[t], r)
        for b in range(halves):
            u = jnp.where(lanes(tile_live, C, r), dot(coup[t, b * C:(b + 1) * C, :], panel[...]), 0.0)
            mids[t, r + b * C:r + (b + 1) * C, :] = (-u).astype(bf16)
        return carry

    lax.fori_loop(0, tiles, refine, 0)
    copies[5].wait()
    copies[6].wait()

    def first(t, carry):
        tile_live = live(tile_ranks[t], r)
        for b in range(chunks):
            sl = slice(b * C, (b + 1) * C)
            ru = row_u[b * per:(b + 1) * per, t].reshape(C, r)
            left = jnp.concatenate([tile_u[t, sl, :], ru], axis=1)
            for q, piece in enumerate(split(dot(left, mids[t]), 2)):
                samp[t, q, sl, :] = piece
        for b in range(halves):
            lo = b * C
            sl = slice(lo, lo + C)
            left = jnp.concatenate([samp[t, 0, :, sl], samp[t, 0, :, sl], samp[t, 1, :, sl], samp[t, 1, :, sl]], axis=0)
            right = jnp.concatenate([samp[t, 0, :, lo:], samp[t, 1, :, lo:], samp[t, 0, :, lo:], samp[t, 1, :, lo:]], axis=0)
            g = dot(left, right, 0, 0)
            down = lax.broadcasted_iota(jnp.int32, g.shape, 0)
            one = (down == lax.broadcasted_iota(jnp.int32, g.shape, 1)) & (down + lo >= tile_live)
            grams[t, sl, lo:] = g + one.astype(f32)
        return carry

    lax.fori_loop(0, tiles, first, 0)

    def factor(t):
        def source(top, lo, hi):
            return grams[t, top:top + B, lo:hi]

        def out_rows(k, lo, value):
            for q, part in enumerate(split(value, 2)):
                fac[t, q, k * B:(k + 1) * B, lo:lo + value.shape[1]] = part

        return factor_inverse(source, work.at[t], diag.at[t], pieces.at[t], out_rows, r, block_inverse)

    drive([factor(t) for t in range(tiles)])

    scale = math.sqrt(n)
    copies[7].wait()

    def last(t, carry):
        tile_live = live(tile_ranks[t], r)
        for h in range(halves):
            hs = slice(h * C, (h + 1) * C)
            k = (h + 1) * C
            right = jnp.concatenate([fac[t, 0, hs, :k], fac[t, 0, hs, :k], fac[t, 1, hs, :k]], axis=1)
            for b in range(chunks):
                sl = slice(b * C, (b + 1) * C)
                left = jnp.concatenate([samp[t, 0, sl, :k], samp[t, 1, sl, :k], samp[t, 0, sl, :k]], axis=1)
                new_u[t, sl, hs] = (dot(left, right, 1, 1) * scale).astype(bf16)
        for b in range(halves):
            sl = slice(b * C, (b + 1) * C)
            v = dot(tile_u[t, :, sl], new_u[t], 0, 0)
            mids[t, sl, :] = jnp.where(subs(tile_live, b * C, C, r), v, 0.0).astype(bf16)
            backs[sl, :] = dot(row_u[:, t, :, sl].reshape(n, C), new_u[t], 0, 0).astype(bf16)
        for b in range(halves):
            sl = slice(b * C, (b + 1) * C)
            mids[t, r + b * C:r + (b + 1) * C, :] = (-dot(coup[t, :, sl], backs[...], 0, 0)).astype(bf16)
        for b in range(chunks):
            sl = slice(b * C, (b + 1) * C)
            left = jnp.concatenate([tile_v[t, sl, :], col_u[sl, :]], axis=1)
            new_v[t, sl, :] = (dot(left, mids[t]) * (1.0 / n)).astype(bf16)
        return carry

    lax.fori_loop(0, tiles, last, 0)


def update_tiles(tile_ranks, tile_u, tile_v, row_u, col_u, sketch, coup, probe):
    tiles, n, r = tile_u.shape
    vmem = pl.BlockSpec(memory_space=pltpu.VMEM)
    return pl.pallas_call(
        update_kernel,
        out_shape=[jax.ShapeDtypeStruct((tiles, n, r), bf16)] * 2,
        in_specs=[pl.BlockSpec(memory_space=pltpu.SMEM)] + [pl.BlockSpec(memory_space=pltpu.HBM)] * 7,
        out_specs=[vmem] * 2,
        scratch_shapes=[
            pltpu.VMEM((tiles, n, r), bf16),
            pltpu.VMEM((tiles, n, r), bf16),
            pltpu.VMEM((16, tiles, n // 16, r), bf16),
            pltpu.VMEM((n, r), bf16),
            pltpu.VMEM((n, r), bf16),
            pltpu.VMEM((tiles, r, r), bf16),
            pltpu.VMEM((r, r), bf16),
            pltpu.VMEM((tiles, 2 * r, r), bf16),
            pltpu.VMEM((tiles, 2, n, r), bf16),
            pltpu.VMEM((tiles, r, r), f32),
            pltpu.VMEM((tiles, r, r), f32),
            pltpu.VMEM((tiles, B, B), f32),
            pltpu.VMEM((tiles, 3, B, r), bf16),
            pltpu.VMEM((tiles, 2, r, r), bf16),
            pltpu.VMEM((r, r), bf16),
            pltpu.SemaphoreType.DMA((8,)),
        ],
        compiler_params=pltpu.CompilerParams(vmem_limit_bytes=58 << 20),
        cost_estimate=pl.CostEstimate(flops=40 * 10**9, bytes_accessed=64 << 20, transcendentals=0),
        name="update_tiles",
    )(tile_ranks, tile_u, tile_v, row_u, col_u, sketch, coup, probe)


def shift(value, axis, step):
    if axis == "z":
        name, pairs = "pcol", [(y * 4 + z, y * 4 + (z + step) % 4) for y in range(4) for z in range(4)]
    elif axis == "y":
        name, pairs = "pcol", [(y * 4 + z, (y + step) % 4 * 4 + z) for y in range(4) for z in range(4)]
    elif axis == "x":
        name, pairs = "prow", [(x * 2 + c, (x + step) % 4 * 2 + c) for x in range(4) for c in range(2)]
    else:
        name, pairs = "prow", [(x * 2 + c, x * 2 + 1 - c) for x in range(4) for c in range(2)]
    return lax.ppermute(value, name, pairs)


def spread(value, axis):
    return [value] + [shift(value, axis, step) for step in (1, 2, 3)]


def on_device(
    tile_u, tile_v, tile_ranks, row_u, row_v, row_ranks, col_u, col_v, col_ranks, diag_tile, sketch
):
    at_row, at_col = lax.axis_index("prow"), lax.axis_index("pcol")
    pos = jnp.stack([at_row // 2, at_row % 2, at_col // 4, at_col % 4]).astype(jnp.int32)
    col_raw = lax.all_gather(col_v[0], "prow", axis=0, tiled=True)
    strip = jnp.stack(spread(diag_tile.T, "z"))
    rows = spread(row_v, "y")
    strip, row_u = lax.optimization_barrier((strip, row_u))
    row_left = lax.all_gather(row_u, "pcol", axis=0, tiled=False)
    strip = jnp.concatenate(spread(strip, "y"), axis=0)
    strip, rows, col_u = lax.optimization_barrier((strip, jnp.stack(rows), col_u))
    col_left = lax.all_gather(col_u[0], "prow", axis=0, tiled=True)
    strips = spread(strip, "x")
    strips = strips + [shift(one, "c", 1) for one in strips]
    rows = spread(rows, "z")
    high, low = diag_inverse(pos, strips)
    tile_u, tile_v, tile_ranks = tile_u[:, 0], tile_v[:, 0], tile_ranks[:, 0]
    coup, probe = couple_tiles(
        pos, tile_ranks, row_ranks, col_ranks, tile_v, rows, col_raw, sketch, high, low
    )
    new_u, new_v = update_tiles(tile_ranks, tile_u, tile_v, row_left, col_left, sketch, coup, probe)
    return new_u[:, None], new_v[:, None]


def solution(mesh):
    in_specs = (
        P("prow", "pcol", None, None),
        P("prow", "pcol", None, None),
        P("prow", "pcol"),
        P("prow", "pcol", None),
        P("prow", "pcol", None),
        P("prow"),
        P("pcol", "prow", None),
        P("pcol", "prow", None),
        P("pcol"),
        P("prow", "pcol"),
        P(),
    )
    out_specs = (P("prow", "pcol", None, None), P("prow", "pcol", None, None))
    return jax.shard_map(
        on_device, mesh=mesh, in_specs=in_specs, out_specs=out_specs, check_vma=False
    )
```

```python
import math

import jax
import jax.numpy as jnp
from jax import lax
from jax.experimental import pallas as pl
from jax.experimental.pallas import tpu as pltpu
from jax.sharding import PartitionSpec as P

B = 128
S = 8
f32 = jnp.float32
bf16 = jnp.bfloat16

def split(x, pieces):
    out = []
    for t in range(pieces):
        part = x.astype(bf16)
        out.append(part)
        if t + 1 < pieces:
            x = x - part.astype(f32)
    return out

def dot(a, b, ca=1, cb=0):
    return lax.dot_general(a, b, (((ca,), (cb,)), ((), ())), preferred_element_type=f32)

def rowb(x, k):
    return jnp.broadcast_to(x[k:k + 1, :], (S, B))

def laneb(x, j):
    return jnp.broadcast_to(x[:, j:j + 1], (S, B))

def solve_back(upper, lines, inverses):
    solved = [None] * S
    for k in reversed(range(S)):
        line = lines[k]
        for m in reversed(range(k + 1, S)):
            line = line - upper[k][m - k - 1] * solved[m]
        solved[k] = line * inverses[k]
    return solved


def eliminate_far(rows, j, solved, inside):
    terms = [laneb(rows, j + k) * solved[k] for k in range(S)]
    while len(terms) > 1:
        terms = [terms[i] + terms[i + 1] for i in range(0, len(terms), 2)]
    return jnp.where(inside, 0.0, rows) - terms[0]


def block_inverse(ref):
    lane = lax.broadcasted_iota(jnp.int32, (S, B), 1)
    sub = lax.broadcasted_iota(jnp.int32, (S, B), 0)
    rows = ref[0:S, :]
    cols = [laneb(rows, k) for k in range(S)]
    for j in range(0, B, S):
        more = j + S < B
        inside = (lane >= j) & (lane < j + S)
        kept = jnp.where(inside, (lane - j == sub).astype(f32), rows)
        if more:
            below = ref[j + S:j + 2 * S, :]
            cross = [laneb(below, j + k) for k in range(S)]
            ahead = [laneb(below, j + S + k) for k in range(S)]
            rest = jnp.where(inside, 0.0, below)
        pivots = None
        upper, lines, inverses = [], [], []
        for k in range(S):
            pivot = rowb(cols[k], k)
            inverse = 1.0 / pivot
            pivots = pivot if pivots is None else jnp.where(sub == k, pivot, pivots)
            across = [rowb(cols[m], k) for m in range(k + 1, S)]
            for m in range(k + 1, S):
                cols[m] = cols[m] - (cols[k] * across[m - k - 1]) * inverse
            line = rowb(kept, k)
            if more:
                weight = cross[k] * inverse
                own = cross[k]
                for m in range(k + 1, S):
                    cross[m] = cross[m] - (own * across[m - k - 1]) * inverse
                for m in range(S):
                    ahead[m] = ahead[m] - (own * rowb(own, m)) * inverse
                rest = rest - weight * line
            kept = kept - jnp.where(sub > k, cols[k], 0.0) * (line * inverse)
            upper.append(across)
            lines.append(line)
            inverses.append(inverse)
        ref[j:j + S, :] = jnp.where(lane <= j + sub, kept * lax.rsqrt(pivots), 0.0)
        if j + 2 * S < B:
            solved = solve_back(upper, lines, inverses)
        for i in range(j + 2 * S, B, S):
            ref[i:i + S, :] = eliminate_far(ref[i:i + S, :], j, solved, inside)
        if more:
            cols, rows = ahead, rest
        yield

def pairs_left(p, axis):
    return jnp.concatenate([p[0], p[0], p[1], p[1], p[0], p[2]], axis=axis)

def pairs_right(p, axis):
    return jnp.concatenate([p[0], p[1], p[0], p[1], p[2], p[0]], axis=axis)

def block_step(k, read, work, diag, pieces, out_rows, n):
    nb = n // B
    r0 = k * B
    own = diag[...]
    own_parts = split(own, 3)
    left = pairs_left(own_parts, 1)

    def line(lo, hi):
        g = dot(left, pairs_right(split(read(r0, lo, hi), 3), 0))
        for t, part in enumerate(split(g, 3)):
            pieces[t, :, lo:hi] = part
        return g

    def shrink(i, lo, hi, zero=False, dest=None):
        a = pairs_left([pieces[t, :, i * B:(i + 1) * B] for t in range(3)], 0)
        b = pairs_right([pieces[t, :, lo:hi] for t in range(3)], 0)
        d = dot(a, b, 0, 0)
        new = -d if zero else read(i * B, lo, hi) - d
        if dest is None:
            work[i * B:(i + 1) * B, lo:hi] = new
        else:
            dest[...] = new

    pending = []
    if k + 1 < nb:
        line(r0 + B, r0 + 2 * B)
        shrink(k + 1, r0 + B, r0 + 2 * B, dest=diag)
        for t, part in enumerate(own_parts):
            pieces[t, :, r0:r0 + B] = part
    out_rows(k, r0, own)
    if k > 0:
        pending.append(lambda: out_rows(k, 0, line(0, r0)))
    if k + 2 < nb:
        pending.append(lambda: line(r0 + 2 * B, n))
    for i in range(k + 1, nb):
        if i > k + 1:
            pending.append(lambda i=i: shrink(i, i * B, n))
        elif i + 1 < nb:
            pending.append(lambda i=i: shrink(i, i * B + B, n))
        pending.append(lambda i=i: shrink(i, r0, r0 + B, zero=True))
        if k > 0:
            pending.append(lambda i=i: shrink(i, 0, r0))
    return pending

def factor_inverse(src, work, diag, pieces, out_rows, n):
    nb = n // B
    diag[...] = src(0, 0, B)

    def again(row, lo, hi):
        return work[row:row + B, lo:hi]

    pending = []
    for k in range(nb):
        step = block_inverse(diag)
        panels = B // S
        done = 0
        for p in range(panels):
            next(step)
            upto = (p + 1) * len(pending) // (panels - 1) if p < panels - 1 else len(pending)
            for t in range(done, min(upto, len(pending))):
                pending[t]()
            done = max(done, min(upto, len(pending)))
            yield
        pending = block_step(k, src if k == 0 else again, work, diag, pieces, out_rows, n)
    for t in pending:
        t()
    yield

def drive(gens):
    gens = list(gens)
    while gens:
        alive = []
        for g in gens:
            try:
                next(g)
                alive.append(g)
            except StopIteration:
                pass
        gens = alive


def piece_slot(pos, index):
    return ((pos[2] - index // 4) & 3) * 4 + ((pos[3] - index % 4) & 3)


def diag_kernel(pos_ref, *refs):
    arrays, (high_out, low_out, high, low, strips, work, diag, pieces, sems) = refs[:8], refs[8:]
    n = high.shape[0]
    copies = [pltpu.make_async_copy(a, strips.at[i], sems.at[i]) for i, a in enumerate(arrays)]
    for copy in copies:
        copy.start()
    high[...] = jnp.zeros(high.shape, bf16)
    low[...] = jnp.zeros(low.shape, bf16)
    pos = [pos_ref[i] for i in range(4)]
    for copy in copies:
        copy.wait()

    def source(row, lo, hi):
        across = []
        for q in range(lo // B, hi // B):
            slot = ((pos[1] + q) & 1) * 4 + ((pos[0] - q // 2) & 3)
            down = [strips[slot, piece_slot(pos, row // 64 + h)] for h in range(2)]
            across.append(jnp.concatenate(down, axis=0))
        return jnp.concatenate(across, axis=1) if len(across) > 1 else across[0]

    def out_rows(k, lo, value):
        parts = split(value, 2)
        for ref, part in zip((high, low), parts):
            ref[k * B:(k + 1) * B, lo:lo + value.shape[1]] = part
        if lo == 0:
            own = pl.ds(k * B, B)
            for h, (ref, out) in enumerate(((high, high_out), (low, low_out))):
                stores.append(pltpu.make_async_copy(ref.at[own], out.at[own], sems.at[8 + 2 * k + h]))
                stores[-1].start()

    stores = []
    drive([factor_inverse(source, work, diag, pieces, out_rows, n)])
    for copy in stores:
        copy.wait()


def diag_inverse(pos, arrays):
    n = 1024
    return pl.pallas_call(
        diag_kernel,
        out_shape=[jax.ShapeDtypeStruct((n, n), bf16)] * 2,
        in_specs=[pl.BlockSpec(memory_space=pltpu.SMEM)] + [pl.BlockSpec(memory_space=pltpu.HBM)] * 8,
        out_specs=[pl.BlockSpec(memory_space=pltpu.HBM)] * 2,
        scratch_shapes=[
            pltpu.VMEM((n, n), bf16),
            pltpu.VMEM((n, n), bf16),
            pltpu.VMEM((8, 16, n // 16, B), f32),
            pltpu.VMEM((n, n), f32),
            pltpu.VMEM((B, B), f32),
            pltpu.VMEM((3, B, n), bf16),
            pltpu.SemaphoreType.DMA((8 + 2 * (n // B),)),
        ],
        compiler_params=pltpu.CompilerParams(vmem_limit_bytes=58 << 20),
        cost_estimate=pl.CostEstimate(flops=40 * 10**9, bytes_accessed=64 << 20, transcendentals=0),
        name="diag_inverse",
    )(pos, *arrays)


C = 256


def live(bucket, r):
    return jnp.left_shift(jnp.int32(r // 8), bucket)


def lanes(count, rows, r):
    return lax.broadcasted_iota(jnp.int32, (rows, r), 1) < count


def subs(count, start, rows, width):
    return lax.broadcasted_iota(jnp.int32, (rows, width), 0) + start < count


def couple_kernel(
    pos_ref, tile_ranks, row_ranks, col_ranks,
    tile_v_in, row_own, row_1, row_2, row_3, col_v_in, sketch_in, high_in, low_in,
    coup, probe,
    tile_v, row_v, col_v, sketch, high, low, row_s, col_s, sems,
):
    n, r = tile_v.shape[1:]
    tiles = tile_v.shape[0]
    chunks = n // C
    strip = row_v.shape[2]
    halves = r // C
    pos = [pos_ref[i] for i in range(4)]
    early = [
        pltpu.make_async_copy(sketch_in, sketch, sems.at[0]),
        pltpu.make_async_copy(tile_v_in, tile_v, sems.at[1]),
    ]
    middle = [
        pltpu.make_async_copy(high_in, high, sems.at[2]),
        pltpu.make_async_copy(low_in, low, sems.at[3]),
        pltpu.make_async_copy(col_v_in, col_v, sems.at[4]),
    ]
    for sz, ref in enumerate((row_own, row_1, row_2, row_3)):
        for sy in range(4):
            place = ((pos[2] - sy) & 3) * 4 + ((pos[3] - sz) & 3)
            middle.append(pltpu.make_async_copy(ref.at[sy], row_v.at[place], sems.at[5 + sz * 4 + sy]))
    for copy in early + middle:
        copy.start()
    for copy in early:
        copy.wait()

    def project(t, carry):
        tile_live = live(tile_ranks[t], r)
        for b in range(halves):
            sl = slice(b * C, (b + 1) * C)
            v = dot(tile_v[t, :, sl], sketch[...], 0, 0)
            keep = subs(tile_live, b * C, C, r) & lanes(tile_live, C, r)
            probe[t, sl, :] = jnp.where(keep, v, 0.0).astype(bf16)
        return carry

    lax.fori_loop(0, tiles, project, 0)
    for copy in middle:
        copy.wait()

    for b in range(chunks):
        k = (b + 1) * C
        left = jnp.concatenate([high[b * C:k, :k], low[b * C:k, :k]], axis=1)

        def solve(t, carry):
            v = row_v[0:k // strip, t].reshape(k, r)
            row_s[t, b * C:k, :] = dot(left, jnp.concatenate([v, v], axis=0)).astype(bf16)
            return carry

        lax.fori_loop(0, tiles, solve, 0)
        v = col_v[0:k, :]
        col_s[b * C:k, :] = dot(left, jnp.concatenate([v, v], axis=0)).astype(bf16)

    col_live = live(col_ranks[0], r)

    def couple(t, carry):
        row_live = live(row_ranks[t], r)
        for b in range(halves):
            sl = slice(b * C, (b + 1) * C)
            c = dot(row_s[t, :, sl], col_s[...], 0, 0)
            keep = subs(row_live, b * C, C, r) & lanes(col_live, C, r)
            coup[t, sl, :] = jnp.where(keep, c, 0.0).astype(bf16)
        return carry

    lax.fori_loop(0, tiles, couple, 0)


def couple_tiles(pos, tile_ranks, row_ranks, col_ranks, tile_v, rows, col_v, sketch, high, low):
    tiles, n, r = tile_v.shape
    smem = pl.BlockSpec(memory_space=pltpu.SMEM)
    vmem = pl.BlockSpec(memory_space=pltpu.VMEM)
    kept = pl.BlockSpec(memory_space=pltpu.HBM)
    return pl.pallas_call(
        couple_kernel,
        out_shape=[jax.ShapeDtypeStruct((tiles, r, r), bf16)] * 2,
        in_specs=[smem] * 4 + [kept] * 9,
        out_specs=[vmem] * 2,
        scratch_shapes=[
            pltpu.VMEM((tiles, n, r), bf16),
            pltpu.VMEM((16, tiles, n // 16, r), bf16),
            pltpu.VMEM((n, r), bf16),
            pltpu.VMEM((n, r), bf16),
            pltpu.VMEM((n, n), bf16),
            pltpu.VMEM((n, n), bf16),
            pltpu.VMEM((tiles, n, r), bf16),
            pltpu.VMEM((n, r), bf16),
            pltpu.SemaphoreType.DMA((21,)),
        ],
        compiler_params=pltpu.CompilerParams(vmem_limit_bytes=58 << 20),
        cost_estimate=pl.CostEstimate(flops=12 * 10**9, bytes_accessed=20 << 20, transcendentals=0),
        name="couple_tiles",
    )(pos, tile_ranks, row_ranks, col_ranks, tile_v, *rows, col_v, sketch, high, low)


def update_kernel(
    tile_ranks,
    tile_u_in, tile_v_in, row_u_in, col_u_in, sketch_in, coup_in, probe_in,
    new_u_out, new_v_out,
    new_u, new_v, tile_u, tile_v, row_u, col_u, sketch, coup,
    panel, mids, samp, grams, work, diag, pieces, fac, backs, sems,
):
    n, r = tile_u.shape[1:]
    tiles = tile_u.shape[0]
    chunks = n // C
    strip = row_u.shape[2]
    per = C // strip
    halves = r // C
    copies = [
        pltpu.make_async_copy(sketch_in, sketch, sems.at[0]),
        pltpu.make_async_copy(col_u_in, col_u, sems.at[1]),
        pltpu.make_async_copy(coup_in, coup, sems.at[2]),
        pltpu.make_async_copy(probe_in.at[0], mids.at[0, 0:r], sems.at[3]),
        pltpu.make_async_copy(probe_in.at[1], mids.at[1, 0:r], sems.at[4]),
        pltpu.make_async_copy(tile_u_in, tile_u, sems.at[5]),
        pltpu.make_async_copy(row_u_in, row_u, sems.at[6]),
        pltpu.make_async_copy(tile_v_in, tile_v, sems.at[7]),
    ]
    for copy in copies:
        copy.start()
    fac[...] = jnp.zeros(fac.shape, bf16)
    copies[0].wait()
    copies[1].wait()
    for b in range(halves):
        sl = slice(b * C, (b + 1) * C)
        panel[sl, :] = dot(col_u[:, sl], sketch[...], 0, 0).astype(bf16)
    copies[2].wait()
    copies[3].wait()
    copies[4].wait()

    def refine(t, carry):
        tile_live = live(tile_ranks[t], r)
        for b in range(halves):
            u = jnp.where(lanes(tile_live, C, r), dot(coup[t, b * C:(b + 1) * C, :], panel[...]), 0.0)
            mids[t, r + b * C:r + (b + 1) * C, :] = (-u).astype(bf16)
        return carry

    lax.fori_loop(0, tiles, refine, 0)
    copies[5].wait()
    copies[6].wait()

    def first(t, carry):
        tile_live = live(tile_ranks[t], r)
        for b in range(chunks):
            sl = slice(b * C, (b + 1) * C)
            ru = row_u[b * per:(b + 1) * per, t].reshape(C, r)
            left = jnp.concatenate([tile_u[t, sl, :], ru], axis=1)
            for q, piece in enumerate(split(dot(left, mids[t]), 2)):
                samp[t, q, sl, :] = piece
        for b in range(halves):
            lo = b * C
            sl = slice(lo, lo + C)
            left = jnp.concatenate([samp[t, 0, :, sl], samp[t, 0, :, sl], samp[t, 1, :, sl], samp[t, 1, :, sl]], axis=0)
            right = jnp.concatenate([samp[t, 0, :, lo:], samp[t, 1, :, lo:], samp[t, 0, :, lo:], samp[t, 1, :, lo:]], axis=0)
            g = dot(left, right, 0, 0)
            down = lax.broadcasted_iota(jnp.int32, g.shape, 0)
            one = (down == lax.broadcasted_iota(jnp.int32, g.shape, 1)) & (down + lo >= tile_live)
            grams[t, sl, lo:] = g + one.astype(f32)
        return carry

    lax.fori_loop(0, tiles, first, 0)

    def factor(t):
        def source(top, lo, hi):
            return grams[t, top:top + B, lo:hi]

        def out_rows(k, lo, value):
            for q, part in enumerate(split(value, 2)):
                fac[t, q, k * B:(k + 1) * B, lo:lo + value.shape[1]] = part

        return factor_inverse(source, work.at[t], diag.at[t], pieces.at[t], out_rows, r)

    drive([factor(t) for t in range(tiles)])

    scale = math.sqrt(n)

    def store(held, out, t, first_sem):
        return pltpu.make_async_copy(held.at[t], out.at[t], sems.at[first_sem + t])

    copies[7].wait()

    def last(t, carry):
        tile_live = live(tile_ranks[t], r)
        for h in range(halves):
            hs = slice(h * C, (h + 1) * C)
            k = (h + 1) * C
            right = jnp.concatenate([fac[t, 0, hs, :k], fac[t, 0, hs, :k], fac[t, 1, hs, :k]], axis=1)
            for b in range(chunks):
                sl = slice(b * C, (b + 1) * C)
                left = jnp.concatenate([samp[t, 0, sl, :k], samp[t, 1, sl, :k], samp[t, 0, sl, :k]], axis=1)
                new_u[t, sl, hs] = (dot(left, right, 1, 1) * scale).astype(bf16)
        store(new_u, new_u_out, t, 8).start()
        for b in range(halves):
            sl = slice(b * C, (b + 1) * C)
            v = dot(tile_u[t, :, sl], new_u[t], 0, 0)
            mids[t, sl, :] = jnp.where(subs(tile_live, b * C, C, r), v, 0.0).astype(bf16)
            backs[sl, :] = dot(row_u[:, t, :, sl].reshape(n, C), new_u[t], 0, 0).astype(bf16)
        for b in range(halves):
            sl = slice(b * C, (b + 1) * C)
            mids[t, r + b * C:r + (b + 1) * C, :] = (-dot(coup[t, :, sl], backs[...], 0, 0)).astype(bf16)
        for b in range(chunks):
            sl = slice(b * C, (b + 1) * C)
            left = jnp.concatenate([tile_v[t, sl, :], col_u[sl, :]], axis=1)
            new_v[t, sl, :] = (dot(left, mids[t]) * (1.0 / n)).astype(bf16)
        store(new_v, new_v_out, t, 10).start()
        return carry

    lax.fori_loop(0, tiles, last, 0)
    for t in range(tiles):
        store(new_u, new_u_out, t, 8).wait()
        store(new_v, new_v_out, t, 10).wait()


def update_tiles(tile_ranks, tile_u, tile_v, row_u, col_u, sketch, coup, probe):
    tiles, n, r = tile_u.shape
    return pl.pallas_call(
        update_kernel,
        out_shape=[jax.ShapeDtypeStruct((tiles, n, r), bf16)] * 2,
        in_specs=[pl.BlockSpec(memory_space=pltpu.SMEM)] + [pl.BlockSpec(memory_space=pltpu.HBM)] * 7,
        out_specs=[pl.BlockSpec(memory_space=pltpu.HBM)] * 2,
        scratch_shapes=[
            pltpu.VMEM((tiles, n, r), bf16),
            pltpu.VMEM((tiles, n, r), bf16),
            pltpu.VMEM((tiles, n, r), bf16),
            pltpu.VMEM((tiles, n, r), bf16),
            pltpu.VMEM((16, tiles, n // 16, r), bf16),
            pltpu.VMEM((n, r), bf16),
            pltpu.VMEM((n, r), bf16),
            pltpu.VMEM((tiles, r, r), bf16),
            pltpu.VMEM((r, r), bf16),
            pltpu.VMEM((tiles, 2 * r, r), bf16),
            pltpu.VMEM((tiles, 2, n, r), bf16),
            pltpu.VMEM((tiles, r, r), f32),
            pltpu.VMEM((tiles, r, r), f32),
            pltpu.VMEM((tiles, B, B), f32),
            pltpu.VMEM((tiles, 3, B, r), bf16),
            pltpu.VMEM((tiles, 2, r, r), bf16),
            pltpu.VMEM((r, r), bf16),
            pltpu.SemaphoreType.DMA((12,)),
        ],
        compiler_params=pltpu.CompilerParams(vmem_limit_bytes=58 << 20),
        cost_estimate=pl.CostEstimate(flops=40 * 10**9, bytes_accessed=64 << 20, transcendentals=0),
        name="update_tiles",
    )(tile_ranks, tile_u, tile_v, row_u, col_u, sketch, coup, probe)


def shift(value, axis, step):
    if axis == "z":
        name, pairs = "pcol", [(y * 4 + z, y * 4 + (z + step) % 4) for y in range(4) for z in range(4)]
    elif axis == "y":
        name, pairs = "pcol", [(y * 4 + z, (y + step) % 4 * 4 + z) for y in range(4) for z in range(4)]
    elif axis == "x":
        name, pairs = "prow", [(x * 2 + c, (x + step) % 4 * 2 + c) for x in range(4) for c in range(2)]
    else:
        name, pairs = "prow", [(x * 2 + c, x * 2 + 1 - c) for x in range(4) for c in range(2)]
    return lax.ppermute(value, name, pairs)


def spread(value, axis):
    return [value] + [shift(value, axis, step) for step in (1, 2, 3)]


def on_device(
    tile_u, tile_v, tile_ranks, row_u, row_v, row_ranks, col_u, col_v, col_ranks, diag_tile, sketch
):
    at_row, at_col = lax.axis_index("prow"), lax.axis_index("pcol")
    pos = jnp.stack([at_row // 2, at_row % 2, at_col // 4, at_col % 4]).astype(jnp.int32)
    row_left = lax.all_gather(row_u, "pcol", axis=0, tiled=False)
    strip = jnp.stack(spread(diag_tile.T, "z"))
    rows = spread(row_v, "y")
    strip = jnp.concatenate(spread(strip, "y"), axis=0)
    strip, rows = lax.optimization_barrier((strip, jnp.stack(rows)))
    strips = spread(strip, "x")
    strips[2], col_u, col_v = lax.optimization_barrier((strips[2], col_u, col_v))
    strips = strips + [shift(one, "c", 1) for one in strips]
    col_raw = lax.all_gather(col_v[0], "prow", axis=0, tiled=True)
    col_left = lax.all_gather(col_u[0], "prow", axis=0, tiled=True)
    rows = spread(rows, "z")
    high, low = diag_inverse(pos, strips)
    tile_u, tile_v, tile_ranks = tile_u[:, 0], tile_v[:, 0], tile_ranks[:, 0]
    coup, probe = couple_tiles(
        pos, tile_ranks, row_ranks, col_ranks, tile_v, rows, col_raw, sketch, high, low
    )
    new_u, new_v = update_tiles(tile_ranks, tile_u, tile_v, row_left, col_left, sketch, coup, probe)
    return new_u[:, None], new_v[:, None]


def solution(mesh):
    in_specs = (
        P("prow", "pcol", None, None),
        P("prow", "pcol", None, None),
        P("prow", "pcol"),
        P("prow", "pcol", None),
        P("prow", "pcol", None),
        P("prow"),
        P("pcol", "prow", None),
        P("pcol", "prow", None),
        P("pcol"),
        P("prow", "pcol"),
        P(),
    )
    out_specs = (P("prow", "pcol", None, None), P("prow", "pcol", None, None))
    return jax.shard_map(
        on_device, mesh=mesh, in_specs=in_specs, out_specs=out_specs, check_vma=False
    )
```
